256 devices in a mesh: span: 8 (over y_lo, x), rows: 32 (over y_hi, z, core).
Axes of the slice: x: 4, y: 4 (y_hi: 2, y_lo: 2; y = y_hi * 2 + y_lo), z: 8, core: 2. Of those that a mesh axis runs over, the one named last changes fastest.
Arguments:
- queries: bfloat16 [1024, 4, 8192], P(('span', 'rows')), may hold values from -150 to 150
- prefix_keys: bfloat16 [1024, 1024], P('span'), may hold values from -6 to 6
- prefix_values: bfloat16 [1024, 1024], P('span'), may hold values from -6 to 6
- prefix_mask: int32 [1024, 8], P(('span', 'rows')), may hold values 0 or 1
- suffix_keys: bfloat16 [512, 512, 1024], P(('span', 'rows')), may hold values from -6 to 6
- suffix_values: bfloat16 [512, 512, 1024], P(('span', 'rows')), may hold values from -6 to 6
- suffix_len: int32 [512], P(('span', 'rows')), may hold values from 1 to 512, 131072 in all
- row_branch: int32 [1024], P(('span', 'rows')), may hold values from 0 to 1
- new_keys: bfloat16 [1024, 4, 1024], P(('span', 'rows')), may hold values from -6 to 6
- new_values: bfloat16 [1024, 4, 1024], P(('span', 'rows')), may hold values from -6 to 6
Outputs:
- attended: bfloat16 [1024, 4, 8192], P(('span', 'rows'))
The draws below stay inside these ranges and needn't reach their ends.
Inputs may be any that keep to these rules, and one draw needn't show every extreme that they name: `suffix_len`: some branch uses all 512 slots.
All inputs are finite; a program needn't handle non-finite values. No bound on the sum of `prefix_mask` or of `suffix_len` on one device may be relied on, other than what follows from the above.
Results may differ from the reference program's by a relative error of at most 0.008.
Values may be sent and summed in bfloat16 or wider, within the bound.
No kernel may reach another device: no remote copies, remote signals or barrier semaphores. Data moves between devices by JAX's collectives and lax.ppermute only.
A program may use at most 64 MiB of HBM per device.

```python
import math
import jax
import jax.numpy as jnp
import numpy as np
from jax import lax

H = 64
KVH = 8
HD = 128
BLK = 128
STEPS = 4
RW_DEV = 4
BR_DEV = 2
SUF = 512
PREFIX = 1024
NB = 8
ROWS = 1024
NBR = 512
N_ROWS = 32


def draw_queries(key, part):
    key = jax.random.fold_in(key, 11)
    full_shape = (ROWS, STEPS, H * HD)
    values = jnp.clip(jax.random.normal(key, full_shape, jnp.float32), -6.0, 6.0)
    return values.astype(jnp.bfloat16)


def touch_ends(values, own_key, least, high):
    longest = values.shape.index(max(values.shape))
    spots = []
    for shift in (0, 1):
        where = [jax.random.randint(jax.random.fold_in(own_key, axis), (), 0, length) for axis, length in enumerate(values.shape)]
        where[longest] = (where[longest] + shift) % values.shape[longest]
        spots.append(tuple(where))
    return values.at[spots[0]].set(least).at[spots[1]].set(high)


def steps_of(rng, extent, shards, low, high):
    loudness, own = 1.0, jax.random.fold_in(rng, 6)
    for position, parts in shards:
        heights = jnp.exp(jax.random.uniform(jax.random.fold_in(own, position), (parts,), jnp.float32, low / len(shards), high / len(shards)))
        loudness = loudness * jnp.repeat(heights, extent[position] // parts).reshape([-1 if axis == position else 1 for axis in range(len(extent))])
    return loudness


def profile(number_of, total, bound, slope):
    portions = [(1 << 20) // math.isqrt(standing ** slope) + 1 for standing in range(2, number_of + 1)]
    spare, holding = total - bound - (number_of - 1), [1] * (number_of - 1)
    while spare > 0:
        movable = [i for i in range(number_of - 1) if holding[i] < bound]
        whole, budget = sum([portions[i] for i in movable]), spare
        for i in movable:
            addition = min(bound - holding[i], max(1, budget * portions[i] // whole), spare)
            holding[i] = holding[i] + addition
            spare = spare - addition
    return np.array([bound] + holding)


def uneven_parts(rng, number_of, total, reach, skew):
    if number_of == 2:
        one = jax.random.randint(rng, (), max(1, total - reach), min(reach, total - 1) + 1)
        return jnp.stack([one, total - one])
    lengths = jnp.asarray(profile(number_of, total, reach, skew), jnp.int32)
    couples = (number_of - 1) // 2
    source_of, receiver = lengths[1:1 + 2 * couples:2], lengths[2:2 + 2 * couples:2]
    margin = jnp.minimum(source_of - 1, reach - receiver)
    shifted = jax.random.randint(jax.random.fold_in(rng, 1), (couples,), 0, 1 << 20) % (margin + 1)
    lengths = lengths.at[1:1 + 2 * couples:2].set(source_of - shifted).at[2:2 + 2 * couples:2].set(receiver + shifted)
    return lengths[jax.random.permutation(jax.random.fold_in(rng, 2), number_of)]


def centred(own_key, dims, scale, reach, cuts=(), kind=jnp.bfloat16):
    factor_of = steps_of(own_key, dims, cuts, -0.22, 0.18) if cuts else 1.0
    entries = jax.random.normal(own_key, dims, jnp.float32) * scale * factor_of
    return jnp.minimum(jnp.maximum(entries, -reach), reach).astype(kind)


def setup_inputs(seed: int = 0) -> dict:
    seeds = jax.random.split(jax.random.key(seed), 11)
    return {
        "queries": draw_queries(jax.random.fold_in(seeds[10], 71), 0),
        "prefix_keys": centred(seeds[1], (PREFIX, KVH * HD), 1.0, 6.0, ((0, 8),)),
        "prefix_values": centred(seeds[2], (PREFIX, KVH * HD), 1.0, 6.0, ((0, 8),)),
        "prefix_mask": touch_ends((jax.random.randint(seeds[3], (ROWS, NB), 0, 2) < 1).astype(jnp.int32), jax.random.fold_in(seeds[3], 1), 0, 1),
        "suffix_keys": centred(seeds[4], (NBR, SUF, KVH * HD), 1.0, 6.0, ((0, 256),)),
        "suffix_values": centred(seeds[5], (NBR, SUF, KVH * HD), 1.0, 6.0, ((0, 256),)),
        "suffix_len": uneven_parts(seeds[6], NBR, NBR * SUF // 2, SUF, 2).astype(jnp.int32),
        "row_branch": touch_ends(jax.random.randint(seeds[7], (ROWS,), 0, BR_DEV), jax.random.fold_in(seeds[7], 1), 0, BR_DEV - 1).astype(jnp.int32),
        "new_keys": centred(seeds[8], (ROWS, STEPS, KVH * HD), 1.0, 6.0, ((0, 256),)),
        "new_values": centred(seeds[9], (ROWS, STEPS, KVH * HD), 1.0, 6.0, ((0, 256),)),
    }


masked_value = -1e30


def reference(queries, prefix_keys, prefix_values, prefix_mask, suffix_keys, suffix_values, suffix_len, row_branch, new_keys, new_values):
    group = H // KVH
    score_scale = HD ** -0.5
    row_ids = jnp.arange(ROWS, dtype=jnp.int32)
    device = row_ids // RW_DEV
    partner = device // N_ROWS * N_ROWS + (device % N_ROWS + N_ROWS // 2) % N_ROWS
    branch_ids = (partner * BR_DEV + row_branch).astype(jnp.int32)
    prefix_key_heads = prefix_keys.astype(jnp.float32).reshape(PREFIX, KVH, HD)
    prefix_value_heads = prefix_values.astype(jnp.float32).reshape(PREFIX, KVH, HD)
    block_of = jnp.arange(PREFIX, dtype=jnp.int32) // BLK
    step_ids = jnp.arange(STEPS, dtype=jnp.int32)
    causal = step_ids[None, :] <= step_ids[:, None]
    slot_ids = jnp.arange(SUF, dtype=jnp.int32)

    def one_row(items):
        query_row, mask_row, branch, key_new, value_new = items
        suffix_k = lax.dynamic_index_in_dim(suffix_keys, branch, 0, keepdims=False)
        suffix_v = lax.dynamic_index_in_dim(suffix_values, branch, 0, keepdims=False)
        length = lax.dynamic_index_in_dim(suffix_len, branch, 0, keepdims=False)
        key_all = jnp.concatenate([prefix_key_heads, suffix_k.astype(jnp.float32).reshape(SUF, KVH, HD), key_new.astype(jnp.float32).reshape(STEPS, KVH, HD)], axis=0)
        value_all = jnp.concatenate([prefix_value_heads, suffix_v.astype(jnp.float32).reshape(SUF, KVH, HD), value_new.astype(jnp.float32).reshape(STEPS, KVH, HD)], axis=0)
        prompt_ok = jnp.broadcast_to((mask_row[block_of] == 1)[None, :], (STEPS, PREFIX))
        suffix_ok = jnp.broadcast_to((slot_ids < length)[None, :], (STEPS, SUF))
        allowed = jnp.concatenate([prompt_ok, suffix_ok, causal], axis=1)[:, None, None, :]
        query_four = query_row.astype(jnp.float32).reshape(STEPS, KVH, group, HD)
        scores = jnp.einsum("tjgd,ljd->tjgl", query_four, key_all, precision=lax.Precision.HIGHEST) * score_scale
        masked = jnp.where(allowed, scores, masked_value)
        largest = jnp.max(masked, axis=-1)
        weights = jnp.where(allowed, jnp.exp(masked - largest[..., None]), 0.0)
        mass = jnp.sum(weights, axis=-1)
        rounded = lax.optimization_barrier(weights.astype(jnp.bfloat16)).astype(jnp.float32)
        mixed = jnp.einsum("tjgl,ljd->tjgd", rounded, value_all, precision=lax.Precision.HIGHEST)
        return (mixed / mass[..., None]).reshape(STEPS, H * HD).astype(jnp.bfloat16)

    return lax.map(one_row, (queries, prefix_mask, branch_ids, new_keys, new_values))
```

```python
import functools

import jax
import jax.numpy as jnp
from jax import lax
from jax.experimental import pallas as pl
from jax.experimental.pallas import tpu as pltpu
from jax.sharding import PartitionSpec as P

H = 64
KVH = 8
HD = 128
GROUP = H // KVH
AXES = ("span", "rows")
MASKED = -1e30
SCALE = 1.4426950408889634 * HD ** (-0.5)
ROWS = 4
STEPS = 4
QR = GROUP * STEPS
NQ = ROWS * QR
TOTAL = KVH * NQ
EXT = 16
STAT = 32


def device_id(x, y, z, c):
    x, y, z, c = x % 4, y % 4, z % 8, c % 2
    return ((y % 2) * 4 + x) * 32 + (y // 2) * 16 + z * 2 + c


def send(value, target):
    pairs = [
        (device_id(x, y, z, c), device_id(*target(x, y, z, c)))
        for x in range(4)
        for y in range(4)
        for z in range(8)
        for c in range(2)
    ]
    return lax.ppermute(value, AXES, pairs)


def to_partner(x, y, z, c):
    return (x, y + 2, z, c)


def to_neighbour(x, y, z, c):
    return (x, y + 1 - 2 * c, z, c)


def from_neighbour(x, y, z, c):
    return (x, y - 1 + 2 * c, z, c)


def along_x(x, y, z, c):
    return (x + 1 - 2 * c, y, z, c)


def across_x(x, y, z, c):
    return (x + 2, y, z, c)


def other_core(x, y, z, c):
    return (x, y, z, 1 - c)


def dot_nt(a, b):
    return lax.dot_general(a, b, (((1,), (1,)), ((), ())), preferred_element_type=jnp.float32)


def dot_nn(a, b):
    return lax.dot_general(a, b, (((1,), (0,)), ((), ())), preferred_element_type=jnp.float32)


def head_rows(ref, j):
    return jnp.concatenate([ref[r * 256 + j * QR : r * 256 + (j + 1) * QR, :] for r in range(ROWS)], axis=0)


def ext_column(q_ref, lane):
    ext = q_ref[TOTAL : TOTAL + ROWS * EXT, :].astype(jnp.float32)
    lanes = lax.broadcasted_iota(jnp.int32, ext.shape, 1)
    column = jnp.sum(jnp.where(lanes == lane, ext, 0.0), axis=1, keepdims=True)
    pieces = []
    for r in range(ROWS):
        piece = column[r * EXT : (r + 1) * EXT, :]
        pieces += [piece, piece]
    return jnp.concatenate(pieces, axis=0)


def pack_stats(stat):
    rows = stat.T[:KVH, :]
    hi = rows.astype(jnp.bfloat16)
    rest = rows - hi.astype(jnp.float32)
    mid = rest.astype(jnp.bfloat16)
    low = (rest - mid.astype(jnp.float32)).astype(jnp.bfloat16)
    pad = jnp.zeros_like(hi)
    return jnp.concatenate([hi, mid, low, pad], axis=0)


def unpack_stats(ref):
    rows = ref[TOTAL : TOTAL + STAT, :].astype(jnp.float32)
    rows = rows[:KVH] + rows[KVH : 2 * KVH] + rows[2 * KVH : 3 * KVH]
    full = jnp.concatenate([rows, jnp.zeros((NQ - KVH, NQ), jnp.float32)], axis=0)
    return full.T


def suffix_kernel(len_ref, q_ref, k_hbm, v_hbm, out_ref, k_buf, v_buf, sems):
    def copies(j):
        cols = slice(j * HD, (j + 1) * HD)
        return (
            pltpu.make_async_copy(k_hbm.at[:, :, cols], k_buf.at[:, :, cols], sems.at[0, j]),
            pltpu.make_async_copy(v_hbm.at[:, :, cols], v_buf.at[:, :, cols], sems.at[1, j]),
        )

    for j in range(KVH):
        for copy in copies(j):
            copy.start()
    slots = k_buf.shape[1]
    second = ext_column(q_ref, KVH) > 0.5
    length = jnp.where(second, len_ref[1], len_ref[0])
    allowed = lax.broadcasted_iota(jnp.int32, (NQ, slots), 1) < length
    lanes = lax.broadcasted_iota(jnp.int32, (NQ, 128), 1)
    stat = jnp.zeros((NQ, 128), jnp.float32)
    for j in range(KVH):
        cols = slice(j * HD, (j + 1) * HD)
        query = head_rows(q_ref, j)
        for copy in copies(j):
            copy.wait()
        scores = jnp.where(second, dot_nt(query, k_buf[1, :, cols]), dot_nt(query, k_buf[0, :, cols]))
        scores = jnp.where(allowed, scores, MASKED)
        largest = jnp.max(scores, axis=1, keepdims=True)
        weights = jnp.exp2((scores - largest) * SCALE)
        mass = jnp.sum(weights, axis=1, keepdims=True)
        rounded = weights.astype(jnp.bfloat16)
        mixed = jnp.where(second, dot_nn(rounded, v_buf[1, :, cols]), dot_nn(rounded, v_buf[0, :, cols]))
        result = (mixed / mass).astype(jnp.bfloat16)
        for r in range(ROWS):
            out_ref[r * 256 + j * QR : r * 256 + (j + 1) * QR, :] = result[r * QR : (r + 1) * QR, :]
        stat = jnp.where(lanes == j, largest * SCALE + jnp.log2(mass), stat)
    out_ref[TOTAL : TOTAL + STAT, :] = pack_stats(stat)


def gather_blocks(refs, k_buf, v_buf, sems, core):
    k_own, v_own, kv_near, kv_far, half_own, half_other = refs
    pairs = [
        (k_own, k_buf.at[0]),
        (v_own, v_buf.at[0]),
        (kv_near.at[0], k_buf.at[1]),
        (kv_near.at[1], v_buf.at[1]),
        (kv_far.at[0], k_buf.at[2]),
        (kv_far.at[1], v_buf.at[2]),
    ]
    copies = [pltpu.make_async_copy(a, b, sems.at[i]) for i, (a, b) in enumerate(pairs)]
    for copy in copies:
        copy.start()

    def halves(k_half, v_half):
        return (
            pltpu.make_async_copy(k_half, k_buf.at[3], sems.at[6]),
            pltpu.make_async_copy(v_half, v_buf.at[3], sems.at[7]),
        )

    @pl.when(core == 0)
    def _():
        for copy in halves(half_own, half_other):
            copy.start()

    @pl.when(core == 1)
    def _():
        for copy in halves(half_other, half_own):
            copy.start()

    for copy in copies:
        copy.wait()
    for copy in halves(half_own, half_other):
        copy.wait()


def prefix_kernel(with_new, *refs):
    if with_new:
        (q_ref, k_own, v_own, kv_near, kv_far, half_own, half_other, nk_ref, nv_ref, out_ref, stat_ref, k_buf, v_buf, sems) = refs
    else:
        (q_ref, k_own, v_own, kv_near, kv_far, half_own, half_other, out_ref, k_buf, v_buf, sems) = refs
    span = lax.axis_index("span")
    core = lax.rem(lax.axis_index("rows"), 2)
    x = lax.rem(span, 4)
    first = span - x
    gather_blocks((k_own, v_own, kv_near, kv_far, half_own, half_other), k_buf, v_buf, sems, core)
    offsets = (0, 3 + 2 * core, 5 - 2 * core, 2)
    allowed = [ext_column(q_ref, first + lax.rem(x + offset, 4)) > 0.5 for offset in offsets]
    lanes = lax.broadcasted_iota(jnp.int32, (NQ, 128), 1)
    stat = jnp.zeros((NQ, 128), jnp.float32)
    if with_new:
        row_of = lax.broadcasted_iota(jnp.int32, (NQ, 128), 0)
        same_row = (row_of // QR) == (lanes // (KVH * STEPS))
        causal = (lanes % STEPS) <= (row_of % STEPS)
        new_base = same_row & causal
        new_head = (lanes // STEPS) % KVH
    for j in range(KVH):
        cols = slice(j * HD, (j + 1) * HD)
        query = head_rows(q_ref, j)
        parts = []
        for i in range(4):
            scores = dot_nt(query, k_buf[i, :, cols])
            parts.append(jnp.where(allowed[i], scores, MASKED))
        if with_new:
            parts.append(jnp.where(new_base & (new_head == j), dot_nt(query, nk_ref[...]), MASKED))
        largest = functools.reduce(jnp.maximum, parts)
        largest = jnp.max(largest, axis=1, keepdims=True)
        weights = [jnp.exp2((part - largest) * SCALE) for part in parts]
        mass = jnp.sum(functools.reduce(jnp.add, weights), axis=1, keepdims=True)
        mixed = functools.reduce(
            jnp.add, [dot_nn(weights[i].astype(jnp.bfloat16), v_buf[i, :, cols]) for i in range(4)]
        )
        if with_new:
            mixed = mixed + dot_nn(weights[4].astype(jnp.bfloat16), nv_ref[...])
        result = (mixed / mass).astype(out_ref.dtype)
        for r in range(ROWS):
            out_ref[r * 256 + j * QR : r * 256 + (j + 1) * QR, :] = result[r * QR : (r + 1) * QR, :]
        stat = jnp.where(lanes == j, largest * SCALE + jnp.log2(mass), stat)
    if with_new:
        stat_ref[...] = stat
    else:
        out_ref[TOTAL : TOTAL + STAT, :] = pack_stats(stat)


def combine_kernel(own_ref, stat_ref, far_ref, near_ref, out_ref):
    own, far, near = stat_ref[...], unpack_stats(far_ref), unpack_stats(near_ref)
    top = jnp.maximum(jnp.maximum(own, far), near)
    own, far, near = jnp.exp2(own - top), jnp.exp2(far - top), jnp.exp2(near - top)
    scale = 1.0 / (own + far + near)
    own, far, near = own * scale, far * scale, near * scale
    for j in range(KVH):
        for r in range(ROWS):
            rows = slice(r * 256 + j * QR, r * 256 + (j + 1) * QR)
            part = slice(r * QR, (r + 1) * QR)
            out_ref[rows, :] = (
                own_ref[rows, :] * own[part, j : j + 1]
                + far_ref[rows, :].astype(jnp.float32) * far[part, j : j + 1]
                + near_ref[rows, :].astype(jnp.float32) * near[part, j : j + 1]
            ).astype(jnp.bfloat16)


VMEM = pl.BlockSpec(memory_space=pltpu.VMEM)
SMEM = pl.BlockSpec(memory_space=pltpu.SMEM)
ANY = pl.BlockSpec(memory_space=pl.ANY)
PACKED = jax.ShapeDtypeStruct((TOTAL + STAT, HD), jnp.bfloat16)


def call(kernel, args, specs, out, scratch, flops):
    return pl.pallas_call(
        kernel,
        out_shape=out,
        in_specs=specs,
        out_specs=jax.tree.map(lambda _: VMEM, out),
        scratch_shapes=scratch,
        cost_estimate=pl.CostEstimate(flops=flops, bytes_accessed=4 << 20, transcendentals=1 << 19),
        compiler_params=pltpu.CompilerParams(vmem_limit_bytes=32 << 20),
    )(*args)


def heads_first(value, heads):
    rows, steps, _ = value.shape
    return value.reshape(rows, steps, heads, HD).transpose(0, 2, 1, 3).reshape(rows * heads * steps, HD)


def on_device(
    queries,
    prefix_keys,
    prefix_values,
    prefix_mask,
    suffix_keys,
    suffix_values,
    suffix_len,
    row_branch,
    new_keys,
    new_values,
):
    core = lax.rem(lax.axis_index("rows"), 2)
    extra = jnp.concatenate([prefix_mask, row_branch[:, None]], axis=1).astype(jnp.bfloat16)
    extra = jnp.pad(extra, ((0, 0), (0, HD - extra.shape[1])))
    extra = jnp.broadcast_to(extra[:, None, :], (ROWS, EXT, HD)).reshape(ROWS * EXT, HD)
    packed = jnp.concatenate([heads_first(queries, H), extra], axis=0)
    far_queries = send(packed, to_partner)
    near_queries = send(packed, to_neighbour)
    both = jnp.stack([prefix_keys, prefix_values])
    kv_near = send(both, along_x)
    half_own = send(lax.dynamic_index_in_dim(both, core, 0, keepdims=False), across_x)
    kv_far = send(kv_near, other_core)
    half_other = send(half_own, other_core)

    suffix = call(
        suffix_kernel,
        (suffix_len, far_queries, suffix_keys, suffix_values),
        [SMEM, VMEM, ANY, ANY],
        PACKED,
        [
            pltpu.VMEM(suffix_keys.shape, jnp.bfloat16),
            pltpu.VMEM(suffix_values.shape, jnp.bfloat16),
            pltpu.SemaphoreType.DMA((2, KVH)),
        ],
        2 << 28,
    )
    suffix = send(suffix, to_partner)

    blocks = (prefix_keys, prefix_values, kv_near, kv_far, half_own, half_other)
    scratch = [
        pltpu.VMEM((4,) + prefix_keys.shape, jnp.bfloat16),
        pltpu.VMEM((4,) + prefix_values.shape, jnp.bfloat16),
        pltpu.SemaphoreType.DMA((8,)),
    ]
    near = call(
        functools.partial(prefix_kernel, False),
        (near_queries,) + blocks,
        [VMEM] + [ANY] * 6,
        PACKED,
        scratch,
        1 << 28,
    )
    near = send(near, from_neighbour)
    own, stat = call(
        functools.partial(prefix_kernel, True),
        (packed,) + blocks + (heads_first(new_keys, KVH), heads_first(new_values, KVH)),
        [VMEM] + [ANY] * 6 + [VMEM] * 2,
        (jax.ShapeDtypeStruct((TOTAL, HD), jnp.float32), jax.ShapeDtypeStruct((NQ, 128), jnp.float32)),
        scratch,
        1 << 28,
    )
    merged = call(
        combine_kernel,
        (own, stat, suffix, near),
        [VMEM] * 4,
        jax.ShapeDtypeStruct((TOTAL, HD), jnp.bfloat16),
        [],
        1 << 20,
    )
    merged = merged.reshape(ROWS, H, STEPS, HD).transpose(0, 2, 1, 3)
    return merged.reshape(queries.shape)


def solution(mesh):
    return jax.shard_map(
        on_device,
        mesh=mesh,
        in_specs=(
            P(AXES, None, None),
            P("span", None),
            P("span", None),
            P(AXES, None),
            P(AXES, None, None),
            P(AXES, None, None),
            P(AXES),
            P(AXES),
            P(AXES, None, None),
            P(AXES, None, None),
        ),
        out_specs=P(AXES, None, None),
        check_vma=False,
    )
```

```python
import functools

import jax
import jax.numpy as jnp
from jax import lax
from jax.experimental import pallas as pl
from jax.experimental.pallas import tpu as pltpu
from jax.sharding import PartitionSpec as P

H = 64
KVH = 8
HD = 128
BLK = 128
GROUP = H // KVH
AXES = ("span", "rows")
MASKED = -1e30
SCALE = 1.4426950408889634 * HD ** (-0.5)
ROWS = 4
STEPS = 4
QR = GROUP * STEPS
NQ = ROWS * QR
TOTAL = KVH * NQ
EXT = 16
STAT = 32


def device_id(x, y, z, c):
    x, y, z, c = x % 4, y % 4, z % 8, c % 2
    return ((y % 2) * 4 + x) * 32 + (y // 2) * 16 + z * 2 + c


def send(value, target):
    pairs = [
        (device_id(x, y, z, c), device_id(*target(x, y, z, c)))
        for x in range(4)
        for y in range(4)
        for z in range(8)
        for c in range(2)
    ]
    return lax.ppermute(value, AXES, pairs)


def to_partner(x, y, z, c):
    return (x, y + 2, z, c)


def to_neighbour(x, y, z, c):
    return (x, y + 1 - 2 * c, z, c)


def from_neighbour(x, y, z, c):
    return (x, y - 1 + 2 * c, z, c)


def along_x(x, y, z, c):
    return (x + 1 - 2 * c, y, z, c)


def other_core(x, y, z, c):
    return (x, y, z, 1 - c)


def dot_nt(a, b):
    return lax.dot_general(a, b, (((1,), (1,)), ((), ())), preferred_element_type=jnp.float32)


def dot_nn(a, b):
    return lax.dot_general(a, b, (((1,), (0,)), ((), ())), preferred_element_type=jnp.float32)


def head_rows(ref, j):
    return jnp.concatenate([ref[r * 256 + j * QR : r * 256 + (j + 1) * QR, :] for r in range(ROWS)], axis=0)


def ext_column(q_ref, lane):
    ext = q_ref[TOTAL : TOTAL + ROWS * EXT, :].astype(jnp.float32)
    lanes = lax.broadcasted_iota(jnp.int32, ext.shape, 1)
    column = jnp.sum(jnp.where(lanes == lane, ext, 0.0), axis=1, keepdims=True)
    pieces = []
    for r in range(ROWS):
        piece = column[r * EXT : (r + 1) * EXT, :]
        pieces += [piece, piece]
    return jnp.concatenate(pieces, axis=0)


def pack_stats(stat):
    rows = stat.T[:KVH, :]
    hi = rows.astype(jnp.bfloat16)
    rest = rows - hi.astype(jnp.float32)
    mid = rest.astype(jnp.bfloat16)
    low = (rest - mid.astype(jnp.float32)).astype(jnp.bfloat16)
    pad = jnp.zeros_like(hi)
    return jnp.concatenate([hi, mid, low, pad], axis=0)


def unpack_stats(ref):
    rows = ref[TOTAL : TOTAL + STAT, :].astype(jnp.float32)
    rows = rows[:KVH] + rows[KVH : 2 * KVH] + rows[2 * KVH : 3 * KVH]
    full = jnp.concatenate([rows, jnp.zeros((NQ - KVH, NQ), jnp.float32)], axis=0)
    return full.T


def pipelined(stages, count):
    held = {}
    for time in range(count + len(stages) - 1):
        for s in range(len(stages)):
            i = time - s
            if 0 <= i < count:
                held[i] = stages[s](i, held.get(i))


def soften(parts):
    largest = jnp.max(functools.reduce(jnp.maximum, parts), axis=1, keepdims=True)
    weights = [jnp.exp2((part - largest) * SCALE) for part in parts]
    mass = jnp.sum(functools.reduce(jnp.add, weights), axis=1, keepdims=True)
    rounded = jnp.concatenate([w.astype(jnp.bfloat16) for w in weights], axis=1)
    return rounded, largest, mass


def store_head(out_ref, j, result):
    for r in range(ROWS):
        out_ref[r * 256 + j * QR : r * 256 + (j + 1) * QR, :] = result[r * QR : (r + 1) * QR, :].astype(out_ref.dtype)


def head(j):
    return slice(j * HD, (j + 1) * HD)


def pack_kernel(
    q_hbm, k_hbm, v_hbm, mask_hbm, branch_hbm, packed_ref, first_ref, second_ref, mask_ref, branch_ref, sems
):
    core = lax.rem(lax.axis_index("rows"), 2)
    small = [
        pltpu.make_async_copy(mask_hbm, mask_ref, sems.at[1]),
        pltpu.make_async_copy(branch_hbm, branch_ref, sems.at[2]),
    ]
    queries = pltpu.make_async_copy(q_hbm, packed_ref.at[pl.ds(0, TOTAL)], sems.at[0])

    def halves(one, two):
        return (pltpu.make_async_copy(one, first_ref, sems.at[3]), pltpu.make_async_copy(two, second_ref, sems.at[4]))

    for copy in small:
        copy.start()
    queries.start()

    @pl.when(core == 0)
    def _():
        for copy in halves(k_hbm, v_hbm):
            copy.start()

    @pl.when(core == 1)
    def _():
        for copy in halves(v_hbm, k_hbm):
            copy.start()

    shape = (ROWS, HD)
    lanes = lax.broadcasted_iota(jnp.int32, shape, 1)
    rows = lax.broadcasted_iota(jnp.int32, shape, 0)
    extra = jnp.zeros(shape, jnp.int32)
    for copy in small:
        copy.wait()
    for i in range(KVH):
        extra = jnp.where(lanes == i, mask_ref[:, i : i + 1], extra)
    for r in range(ROWS):
        extra = jnp.where((lanes == KVH) & (rows == r), branch_ref[:, r : r + 1], extra)
    extra = extra.astype(jnp.float32)
    for r in range(ROWS):
        tile = jnp.broadcast_to(extra[r : r + 1, :], (EXT, HD)).astype(jnp.bfloat16)
        packed_ref[TOTAL + r * EXT : TOTAL + (r + 1) * EXT, :] = tile
    queries.wait()
    for copy in halves(k_hbm, v_hbm):
        copy.wait()


def load_kernel(*refs):
    count = len(refs) // 2
    sems = refs[-1]
    copies = [pltpu.make_async_copy(refs[i], refs[count + i], sems.at[i]) for i in range(count)]
    for copy in copies:
        copy.start()
    for copy in copies:
        copy.wait()


def suffix_kernel(len_ref, q_ref, k_ref, v_ref, out_ref):
    slots = k_ref.shape[1]
    second = ext_column(q_ref, KVH) > 0.5
    wide = jnp.broadcast_to(second, (NQ, HD))
    length = jnp.where(second, len_ref[:, 1:2], len_ref[:, 0:1])
    allowed = lax.broadcasted_iota(jnp.int32, (NQ, slots), 1) < length
    lanes = lax.broadcasted_iota(jnp.int32, (NQ, 128), 1)
    zero = jnp.zeros((NQ, HD), jnp.bfloat16)
    stats = [jnp.zeros((NQ, 128), jnp.float32)]

    def score(j, _):
        query = head_rows(q_ref, j)
        query = jnp.concatenate([jnp.where(wide, zero, query), jnp.where(wide, query, zero)], axis=1)
        return dot_nt(query, jnp.concatenate([k_ref[0, :, head(j)], k_ref[1, :, head(j)]], axis=1))

    def weigh(j, scores):
        return soften([jnp.where(allowed, scores, MASKED)])

    def mix(j, held):
        rounded, largest, mass = held
        mixed = dot_nn(rounded, jnp.concatenate([v_ref[0, :, head(j)], v_ref[1, :, head(j)]], axis=1))
        mixed = jnp.where(second, mixed[:, HD:], mixed[:, :HD])
        store_head(out_ref, j, mixed * (1.0 / mass))
        stats[0] = jnp.where(lanes == j, largest * SCALE + jnp.log2(mass), stats[0])

    pipelined((score, weigh, mix), KVH)
    out_ref[TOTAL : TOTAL + STAT, :] = pack_stats(stats[0])


def prefix_kernel(with_new, *refs):
    q_ref, k_own, v_own, near_one, near_two, far_one, far_two, half_own, half_other = refs[:9]
    if with_new:
        nk_ref, nv_ref, out_ref, stat_ref = refs[9:]
    else:
        (out_ref,) = refs[9:]
    span = lax.axis_index("span")
    core = lax.rem(lax.axis_index("rows"), 2)
    x = lax.rem(span, 4)
    first = span - x
    allowed = [ext_column(q_ref, first + lax.rem(x + offset, 4)) > 0.5 for offset in (0, 3, 1, 2)]
    lanes = lax.broadcasted_iota(jnp.int32, (NQ, 128), 1)
    on_second = jnp.full((BLK, HD), core) == 1
    stats = [jnp.zeros((NQ, 128), jnp.float32)]
    if with_new:
        row_of = lax.broadcasted_iota(jnp.int32, (NQ, 128), 0)
        same_row = (row_of // QR) == (lanes // (KVH * STEPS))
        new_base = same_row & ((lanes % STEPS) <= (row_of % STEPS))
        new_head = (lanes // STEPS) % KVH

    def by_core(j, zero, one):
        return jnp.where(on_second, one[:, head(j)], zero[:, head(j)])

    def score(j, _):
        keys = [
            k_own[:, head(j)],
            by_core(j, near_one, far_one),
            by_core(j, far_two, near_two),
            by_core(j, half_own, half_other),
        ]
        if with_new:
            keys.append(nk_ref[...])
        return dot_nt(head_rows(q_ref, j), jnp.concatenate(keys, axis=0))

    def weigh(j, scores):
        parts = [jnp.where(allowed[i], scores[:, i * BLK : (i + 1) * BLK], MASKED) for i in range(4)]
        if with_new:
            parts.append(jnp.where(new_base & (new_head == j), scores[:, 4 * BLK :], MASKED))
        return soften(parts)

    def mix(j, held):
        rounded, largest, mass = held
        values = [
            v_own[:, head(j)],
            by_core(j, near_two, far_two),
            by_core(j, far_one, near_one),
            by_core(j, half_other, half_own),
        ]
        if with_new:
            values.append(nv_ref[...])
        mixed = dot_nn(rounded, jnp.concatenate(values, axis=0))
        store_head(out_ref, j, mixed * (1.0 / mass))
        stats[0] = jnp.where(lanes == j, largest * SCALE + jnp.log2(mass), stats[0])

    pipelined((score, weigh, mix), KVH)
    if with_new:
        stat_ref[...] = stats[0]
    else:
        out_ref[TOTAL : TOTAL + STAT, :] = pack_stats(stats[0])


def combine_kernel(own_ref, stat_ref, far_ref, near_ref, out_ref):
    own, far, near = stat_ref[...], unpack_stats(far_ref), unpack_stats(near_ref)
    top = jnp.maximum(jnp.maximum(own, far), near)
    own, far, near = jnp.exp2(own - top), jnp.exp2(far - top), jnp.exp2(near - top)
    scale = 1.0 / (own + far + near)
    own, far, near = own * scale, far * scale, near * scale
    for j in range(KVH):
        for r in range(ROWS):
            rows = slice(r * 256 + j * QR, r * 256 + (j + 1) * QR)
            part = slice(r * QR, (r + 1) * QR)
            out_ref[rows, :] = (
                own_ref[rows, :] * own[part, j : j + 1]
                + far_ref[rows, :].astype(jnp.float32) * far[part, j : j + 1]
                + near_ref[rows, :].astype(jnp.float32) * near[part, j : j + 1]
            ).astype(jnp.bfloat16)


VMEM = pl.BlockSpec(memory_space=pltpu.VMEM)
HBM = pl.BlockSpec(memory_space=pltpu.HBM)


def vmem(shape, dtype=jnp.bfloat16):
    return pltpu.VMEM(shape, dtype)


PACKED = vmem((TOTAL + STAT, HD))


def in_hbm(*values):
    return tuple(pltpu.with_memory_space_constraint(value, pltpu.HBM) for value in values)


def call(kernel, args, specs, out, scratch=()):
    return pl.pallas_call(
        kernel,
        out_shape=out,
        in_specs=specs,
        out_specs=jax.tree.map(lambda _: VMEM, out),
        scratch_shapes=list(scratch),
        cost_estimate=pl.CostEstimate(flops=1, bytes_accessed=1, transcendentals=0),
        compiler_params=pltpu.CompilerParams(vmem_limit_bytes=16 << 20),
    )(*args)


def heads_first(value, heads):
    rows, steps, _ = value.shape
    return value.reshape(rows, steps, heads, HD).transpose(0, 2, 1, 3).reshape(rows * heads * steps, HD)


def on_device(
    queries,
    prefix_keys,
    prefix_values,
    prefix_mask,
    suffix_keys,
    suffix_values,
    suffix_len,
    row_branch,
    new_keys,
    new_values,
):
    block = prefix_keys.shape
    packed, one, two = call(
        pack_kernel,
        in_hbm(heads_first(queries, H), prefix_keys, prefix_values, prefix_mask, row_branch.reshape(1, ROWS)),
        [HBM] * 5,
        (vmem((TOTAL + ROWS * EXT, HD)), vmem(block), vmem(block)),
        [
            pltpu.VMEM(prefix_mask.shape, jnp.int32),
            pltpu.VMEM((1, ROWS), jnp.int32),
            pltpu.SemaphoreType.DMA((5,)),
        ],
    )
    near_one = send(one, along_x)
    far_queries = send(packed, to_partner)
    near_two = send(two, along_x)
    half_own = send(near_one, along_x)
    far_one = send(near_one, other_core)
    far_two = send(near_two, other_core)

    stored = (suffix_len.reshape(1, 2), suffix_keys, suffix_values)
    stored, packed = lax.optimization_barrier((stored, packed))
    stored = call(
        load_kernel,
        in_hbm(*stored),
        [HBM] * 3,
        tuple(vmem(value.shape, value.dtype) for value in stored),
        [pltpu.SemaphoreType.DMA((3,))],
    )
    later, _ = lax.optimization_barrier((packed, near_one))
    near_queries = send(later, to_neighbour)
    suffix = call(suffix_kernel, (stored[0], far_queries, stored[1], stored[2]), [VMEM] * 4, PACKED)
    half_own, _ = lax.optimization_barrier((half_own, suffix))
    half_other = send(half_own, other_core)
    suffix = send(suffix, to_partner)

    blocks = (prefix_keys, prefix_values, near_one, near_two, far_one, far_two, half_own, half_other)
    near = call(functools.partial(prefix_kernel, False), (near_queries,) + blocks, [VMEM] * 9, PACKED)
    near = send(near, from_neighbour)
    own, stat = call(
        functools.partial(prefix_kernel, True),
        (packed,) + blocks + (heads_first(new_keys, KVH), heads_first(new_values, KVH)),
        [VMEM] * 11,
        (vmem((TOTAL, HD), jnp.float32), vmem((NQ, 128), jnp.float32)),
    )
    merged = call(
        combine_kernel, (own, stat, suffix, near), [VMEM] * 4, jax.ShapeDtypeStruct((TOTAL, HD), jnp.bfloat16)
    )
    merged = merged.reshape(ROWS, H, STEPS, HD).transpose(0, 2, 1, 3)
    return merged.reshape(queries.shape)


def solution(mesh):
    return jax.shard_map(
        on_device,
        mesh=mesh,
        in_specs=(
            P(AXES, None, None),
            P("span", None),
            P("span", None),
            P(AXES, None),
            P(AXES, None, None),
            P(AXES, None, None),
            P(AXES),
            P(AXES),
            P(AXES, None, None),
            P(AXES, None, None),
        ),
        out_specs=P(AXES, None, None),
        check_vma=False,
    )
```

```python
import functools

import jax
import jax.numpy as jnp
from jax import lax
from jax.experimental import pallas as pl
from jax.experimental.pallas import tpu as pltpu
from jax.sharding import PartitionSpec as P

H = 64
KVH = 8
HD = 128
BLK = 128
GROUP = H // KVH
AXES = ("span", "rows")
MASKED = -1e30
SCALE = 1.4426950408889634 * HD ** (-0.5)
ROWS = 4
STEPS = 4
QR = GROUP * STEPS
NQ = ROWS * QR
TOTAL = KVH * NQ
EXT = 16
STAT = 32


def device_id(x, y, z, c):
    x, y, z, c = x % 4, y % 4, z % 8, c % 2
    return ((y % 2) * 4 + x) * 32 + (y // 2) * 16 + z * 2 + c


def send(value, target):
    pairs = [
        (device_id(x, y, z, c), device_id(*target(x, y, z, c)))
        for x in range(4)
        for y in range(4)
        for z in range(8)
        for c in range(2)
    ]
    return lax.ppermute(value, AXES, pairs)


def to_partner(x, y, z, c):
    return (x, y + 2, z, c)


def to_neighbour(x, y, z, c):
    return (x, y + 1 - 2 * c, z, c)


def from_neighbour(x, y, z, c):
    return (x, y - 1 + 2 * c, z, c)


def along_x(x, y, z, c):
    return (x + 1 - 2 * c, y, z, c)


def other_core(x, y, z, c):
    return (x, y, z, 1 - c)


def dot_nt(a, b):
    return lax.dot_general(a, b, (((1,), (1,)), ((), ())), preferred_element_type=jnp.float32)


def dot_nn(a, b):
    return lax.dot_general(a, b, (((1,), (0,)), ((), ())), preferred_element_type=jnp.float32)


def head_rows(ref, j):
    return jnp.concatenate([ref[r * 256 + j * QR : r * 256 + (j + 1) * QR, :] for r in range(ROWS)], axis=0)


def ext_column(q_ref, lane):
    ext = q_ref[TOTAL : TOTAL + ROWS * EXT, :].astype(jnp.float32)
    lanes = lax.broadcasted_iota(jnp.int32, ext.shape, 1)
    column = jnp.sum(jnp.where(lanes == lane, ext, 0.0), axis=1, keepdims=True)
    pieces = []
    for r in range(ROWS):
        piece = column[r * EXT : (r + 1) * EXT, :]
        pieces += [piece, piece]
    return jnp.concatenate(pieces, axis=0)


def pack_stats(stat):
    rows = stat.T[:KVH, :]
    hi = rows.astype(jnp.bfloat16)
    rest = rows - hi.astype(jnp.float32)
    mid = rest.astype(jnp.bfloat16)
    low = (rest - mid.astype(jnp.float32)).astype(jnp.bfloat16)
    pad = jnp.zeros_like(hi)
    return jnp.concatenate([hi, mid, low, pad], axis=0)


def unpack_stats(ref):
    rows = ref[TOTAL : TOTAL + STAT, :].astype(jnp.float32)
    rows = rows[:KVH] + rows[KVH : 2 * KVH] + rows[2 * KVH : 3 * KVH]
    full = jnp.concatenate([rows, jnp.zeros((NQ - KVH, NQ), jnp.float32)], axis=0)
    return full.T


def pipelined(stages, count):
    held = {}
    for time in range(count + len(stages) - 1):
        for s in range(len(stages)):
            i = time - s
            if 0 <= i < count:
                held[i] = stages[s](i, held.get(i))


def soften(parts):
    largest = jnp.max(functools.reduce(jnp.maximum, parts), axis=1, keepdims=True)
    weights = [jnp.exp2((part - largest) * SCALE) for part in parts]
    mass = jnp.sum(functools.reduce(jnp.add, weights), axis=1, keepdims=True)
    rounded = jnp.concatenate([w.astype(jnp.bfloat16) for w in weights], axis=1)
    return rounded, largest, mass


def store_head(out_ref, j, result):
    for r in range(ROWS):
        out_ref[r * 256 + j * QR : r * 256 + (j + 1) * QR, :] = result[r * QR : (r + 1) * QR, :].astype(out_ref.dtype)


def head(j):
    return slice(j * HD, (j + 1) * HD)


def pack_kernel(q_hbm, mask_hbm, branch_hbm, packed_ref, mask_ref, branch_ref, sems):
    queries = pltpu.make_async_copy(q_hbm, packed_ref.at[pl.ds(0, TOTAL)], sems.at[0])
    small = [
        pltpu.make_async_copy(mask_hbm, mask_ref, sems.at[1]),
        pltpu.make_async_copy(branch_hbm, branch_ref, sems.at[2]),
    ]
    for copy in small + [queries]:
        copy.start()
    shape = (ROWS, HD)
    lanes = lax.broadcasted_iota(jnp.int32, shape, 1)
    rows = lax.broadcasted_iota(jnp.int32, shape, 0)
    extra = jnp.zeros(shape, jnp.int32)
    for copy in small:
        copy.wait()
    for i in range(KVH):
        extra = jnp.where(lanes == i, mask_ref[:, i : i + 1], extra)
    for r in range(ROWS):
        extra = jnp.where((lanes == KVH) & (rows == r), branch_ref[:, r : r + 1], extra)
    extra = extra.astype(jnp.float32)
    for r in range(ROWS):
        tile = jnp.broadcast_to(extra[r : r + 1, :], (EXT, HD)).astype(jnp.bfloat16)
        packed_ref[TOTAL + r * EXT : TOTAL + (r + 1) * EXT, :] = tile
    queries.wait()


def load_kernel(*refs):
    count = len(refs) // 2
    sems = refs[-1]
    copies = [pltpu.make_async_copy(refs[i], refs[count + i], sems.at[i]) for i in range(count)]
    for copy in copies:
        copy.start()
    for copy in copies:
        copy.wait()


def suffix_kernel(len_ref, q_ref, k_ref, v_ref, out_ref):
    slots = k_ref.shape[1]
    second = ext_column(q_ref, KVH) > 0.5
    wide = jnp.broadcast_to(second, (NQ, HD))
    length = jnp.where(second, len_ref[:, 1:2], len_ref[:, 0:1])
    allowed = lax.broadcasted_iota(jnp.int32, (NQ, slots), 1) < length
    lanes = lax.broadcasted_iota(jnp.int32, (NQ, 128), 1)
    zero = jnp.zeros((NQ, HD), jnp.bfloat16)
    stats = [jnp.zeros((NQ, 128), jnp.float32)]

    def score(j, _):
        query = head_rows(q_ref, j)
        query = jnp.concatenate([jnp.where(wide, zero, query), jnp.where(wide, query, zero)], axis=1)
        return dot_nt(query, jnp.concatenate([k_ref[0, :, head(j)], k_ref[1, :, head(j)]], axis=1))

    def weigh(j, scores):
        return soften([jnp.where(allowed, scores, MASKED)])

    def mix(j, held):
        rounded, largest, mass = held
        mixed = dot_nn(rounded, jnp.concatenate([v_ref[0, :, head(j)], v_ref[1, :, head(j)]], axis=1))
        mixed = jnp.where(second, mixed[:, HD:], mixed[:, :HD])
        store_head(out_ref, j, mixed * (1.0 / mass))
        stats[0] = jnp.where(lanes == j, largest * SCALE + jnp.log2(mass), stats[0])

    pipelined((score, weigh, mix), KVH)
    out_ref[TOTAL : TOTAL + STAT, :] = pack_stats(stats[0])


def prefix_kernel(with_new, *refs):
    q_ref, k_own, v_own, k_near, v_near, k_far, v_far, k_next, v_next = refs[:9]
    if with_new:
        nk_ref, nv_ref, out_ref, stat_ref = refs[9:]
    else:
        (out_ref,) = refs[9:]
    span = lax.axis_index("span")
    core = lax.rem(lax.axis_index("rows"), 2)
    x = lax.rem(span, 4)
    first = span - x
    offsets = (0, 3 + 2 * core, 5 - 2 * core, 2)
    allowed = [ext_column(q_ref, first + lax.rem(x + offset, 4)) > 0.5 for offset in offsets]
    lanes = lax.broadcasted_iota(jnp.int32, (NQ, 128), 1)
    stats = [jnp.zeros((NQ, 128), jnp.float32)]
    if with_new:
        row_of = lax.broadcasted_iota(jnp.int32, (NQ, 128), 0)
        same_row = (row_of // QR) == (lanes // (KVH * STEPS))
        new_base = same_row & ((lanes % STEPS) <= (row_of % STEPS))
        new_head = (lanes // STEPS) % KVH

    def score(j, _):
        keys = [ref[:, head(j)] for ref in (k_own, k_near, k_far, k_next)]
        if with_new:
            keys.append(nk_ref[...])
        return dot_nt(head_rows(q_ref, j), jnp.concatenate(keys, axis=0))

    def weigh(j, scores):
        parts = [jnp.where(allowed[i], scores[:, i * BLK : (i + 1) * BLK], MASKED) for i in range(4)]
        if with_new:
            parts.append(jnp.where(new_base & (new_head == j), scores[:, 4 * BLK :], MASKED))
        return soften(parts)

    def mix(j, held):
        rounded, largest, mass = held
        values = [ref[:, head(j)] for ref in (v_own, v_near, v_far, v_next)]
        if with_new:
            values.append(nv_ref[...])
        mixed = dot_nn(rounded, jnp.concatenate(values, axis=0))
        store_head(out_ref, j, mixed * (1.0 / mass))
        stats[0] = jnp.where(lanes == j, largest * SCALE + jnp.log2(mass), stats[0])

    pipelined((score, weigh, mix), KVH)
    if with_new:
        stat_ref[...] = stats[0]
    else:
        out_ref[TOTAL : TOTAL + STAT, :] = pack_stats(stats[0])


def merge_kernel(own_ref, stat_ref, other_ref, out_ref, *merged_stat):
    own, other = stat_ref[...], unpack_stats(other_ref)
    top = jnp.maximum(own, other)
    mass = jnp.exp2(own - top) + jnp.exp2(other - top)
    share = jnp.exp2(own - top) / mass
    for ref in merged_stat:
        ref[...] = top + jnp.log2(mass)
    for j in range(KVH):
        for r in range(ROWS):
            rows = slice(r * 256 + j * QR, r * 256 + (j + 1) * QR)
            second = other_ref[rows, :].astype(jnp.float32)
            weight = share[r * QR : (r + 1) * QR, j : j + 1]
            out_ref[rows, :] = (second + (own_ref[rows, :] - second) * weight).astype(out_ref.dtype)


VMEM = pl.BlockSpec(memory_space=pltpu.VMEM)
HBM = pl.BlockSpec(memory_space=pltpu.HBM)


def vmem(shape, dtype=jnp.bfloat16):
    return pltpu.VMEM(shape, dtype)


PACKED = vmem((TOTAL + STAT, HD))


def in_hbm(*values):
    return tuple(pltpu.with_memory_space_constraint(value, pltpu.HBM) for value in values)


def call(kernel, args, specs, out, scratch=()):
    return pl.pallas_call(
        kernel,
        out_shape=out,
        in_specs=specs,
        out_specs=jax.tree.map(lambda _: VMEM, out),
        scratch_shapes=list(scratch),
        cost_estimate=pl.CostEstimate(flops=1, bytes_accessed=1, transcendentals=0),
        compiler_params=pltpu.CompilerParams(vmem_limit_bytes=16 << 20),
    )(*args)


def heads_first(value, heads):
    rows, steps, _ = value.shape
    return value.reshape(rows, steps, heads, HD).transpose(0, 2, 1, 3).reshape(rows * heads * steps, HD)


def on_device(
    queries,
    prefix_keys,
    prefix_values,
    prefix_mask,
    suffix_keys,
    suffix_values,
    suffix_len,
    row_branch,
    new_keys,
    new_values,
):
    packed = call(
        pack_kernel,
        in_hbm(heads_first(queries, H), prefix_mask, row_branch.reshape(1, ROWS)),
        [HBM] * 3,
        vmem((TOTAL + ROWS * EXT, HD)),
        [
            pltpu.VMEM(prefix_mask.shape, jnp.int32),
            pltpu.VMEM((1, ROWS), jnp.int32),
            pltpu.SemaphoreType.DMA((3,)),
        ],
    )
    near_one = send(lax.optimization_barrier((prefix_keys, packed))[0], along_x)
    far_queries = send(packed, to_partner)
    near_two = send(lax.optimization_barrier((prefix_values, packed))[0], along_x)
    stored = (suffix_len.reshape(1, 2), suffix_keys, suffix_values)
    stored = lax.optimization_barrier((stored, packed))[0]
    stored = call(
        load_kernel,
        in_hbm(*stored),
        [HBM] * 3,
        tuple(vmem(value.shape, value.dtype) for value in stored),
        [pltpu.SemaphoreType.DMA((3,))],
    )
    next_one = send(lax.optimization_barrier((near_one, stored[0]))[0], along_x)
    next_two = send(lax.optimization_barrier((near_two, stored[0]))[0], along_x)
    far_one = send(lax.optimization_barrier((near_one, stored[0]))[0], other_core)
    far_two = send(lax.optimization_barrier((near_two, stored[0]))[0], other_core)
    near_queries = send(lax.optimization_barrier((packed, near_one, stored[0]))[0], to_neighbour)
    suffix = call(suffix_kernel, (stored[0], far_queries, stored[1], stored[2]), [VMEM] * 4, PACKED)
    suffix = send(suffix, to_partner)

    blocks = (prefix_keys, prefix_values, near_one, near_two, far_one, far_two, next_one, next_two)
    near = call(functools.partial(prefix_kernel, False), (near_queries,) + blocks, [VMEM] * 9, PACKED)
    near = send(near, from_neighbour)
    partial = (vmem((TOTAL, HD), jnp.float32), vmem((NQ, 128), jnp.float32))
    own, stat = call(
        functools.partial(prefix_kernel, True),
        (packed,) + blocks + (heads_first(new_keys, KVH), heads_first(new_values, KVH)),
        [VMEM] * 11,
        partial,
    )
    own, stat = call(merge_kernel, (own, stat, suffix), [VMEM] * 3, partial)
    merged = call(merge_kernel, (own, stat, near), [VMEM] * 3, jax.ShapeDtypeStruct((TOTAL, HD), jnp.bfloat16))
    merged = merged.reshape(ROWS, H, STEPS, HD).transpose(0, 2, 1, 3)
    return merged.reshape(queries.shape)


def solution(mesh):
    return jax.shard_map(
        on_device,
        mesh=mesh,
        in_specs=(
            P(AXES, None, None),
            P("span", None),
            P("span", None),
            P(AXES, None),
            P(AXES, None, None),
            P(AXES, None, None),
            P(AXES),
            P(AXES),
            P(AXES, None, None),
            P(AXES, None, None),
        ),
        out_specs=P(AXES, None, None),
        check_vma=False,
    )
```

```python
import functools

import jax
import jax.numpy as jnp
from jax import lax
from jax.experimental import pallas as pl
from jax.experimental.pallas import tpu as pltpu
from jax.sharding import PartitionSpec as P

H = 64
KVH = 8
HD = 128
BLK = 128
GROUP = H // KVH
AXES = ("span", "rows")
MASKED = -1e30
SCALE = 1.4426950408889634 * HD ** (-0.5)
ROWS = 4
STEPS = 4
QR = GROUP * STEPS
NQ = ROWS * QR
TOTAL = KVH * NQ
EXT = 16
STAT = 32


def device_id(x, y, z, c):
    x, y, z, c = x % 4, y % 4, z % 8, c % 2
    return ((y % 2) * 4 + x) * 32 + (y // 2) * 16 + z * 2 + c


def send(value, target):
    pairs = [
        (device_id(x, y, z, c), device_id(*target(x, y, z, c)))
        for x in range(4)
        for y in range(4)
        for z in range(8)
        for c in range(2)
    ]
    return lax.ppermute(value, AXES, pairs)


def after(value, *others):
    return lax.optimization_barrier((value, *others))[0]


def to_partner(x, y, z, c):
    return (x, y + 2, z, c)


def to_neighbour(x, y, z, c):
    return (x, y + 1 - 2 * c, z, c)


def from_neighbour(x, y, z, c):
    return (x, y - 1 + 2 * c, z, c)


def along_x(x, y, z, c):
    return (x + 1 - 2 * c, y, z, c)


def other_core(x, y, z, c):
    return (x, y, z, 1 - c)


def dot_nt(a, b):
    return lax.dot_general(a, b, (((1,), (1,)), ((), ())), preferred_element_type=jnp.float32)


def dot_nn(a, b):
    return lax.dot_general(a, b, (((1,), (0,)), ((), ())), preferred_element_type=jnp.float32)


def head_rows(ref, j):
    return jnp.concatenate([ref[r * 256 + j * QR : r * 256 + (j + 1) * QR, :] for r in range(ROWS)], axis=0)


def ext_column(q_ref, lane):
    ext = q_ref[TOTAL : TOTAL + ROWS * EXT, :].astype(jnp.float32)
    lanes = lax.broadcasted_iota(jnp.int32, ext.shape, 1)
    column = jnp.sum(jnp.where(lanes == lane, ext, 0.0), axis=1, keepdims=True)
    pieces = []
    for r in range(ROWS):
        piece = column[r * EXT : (r + 1) * EXT, :]
        pieces += [piece, piece]
    return jnp.concatenate(pieces, axis=0)


def pack_stats(stat):
    rows = stat.T[:KVH, :]
    hi = rows.astype(jnp.bfloat16)
    rest = rows - hi.astype(jnp.float32)
    mid = rest.astype(jnp.bfloat16)
    low = (rest - mid.astype(jnp.float32)).astype(jnp.bfloat16)
    pad = jnp.zeros_like(hi)
    return jnp.concatenate([hi, mid, low, pad], axis=0)


def unpack_stats(ref):
    rows = ref[TOTAL : TOTAL + STAT, :].astype(jnp.float32)
    rows = rows[:KVH] + rows[KVH : 2 * KVH] + rows[2 * KVH : 3 * KVH]
    full = jnp.concatenate([rows, jnp.zeros((NQ - KVH, NQ), jnp.float32)], axis=0)
    return full.T


def pipelined(stages, count):
    held = {}
    for time in range(count + len(stages) - 1):
        for s in range(len(stages)):
            i = time - s
            if 0 <= i < count:
                held[i] = stages[s](i, held.get(i))


def soften(parts):
    largest = jnp.max(functools.reduce(jnp.maximum, parts), axis=1, keepdims=True)
    weights = [jnp.exp2((part - largest) * SCALE) for part in parts]
    mass = jnp.sum(functools.reduce(jnp.add, weights), axis=1, keepdims=True)
    rounded = jnp.concatenate([w.astype(jnp.bfloat16) for w in weights], axis=1)
    return rounded, largest, mass


def store_head(out_ref, j, result):
    for r in range(ROWS):
        out_ref[r * 256 + j * QR : r * 256 + (j + 1) * QR, :] = result[r * QR : (r + 1) * QR, :].astype(out_ref.dtype)


def head(j):
    return slice(j * HD, (j + 1) * HD)


def pack_kernel(q_hbm, mask_hbm, branch_hbm, packed_ref, mask_ref, branch_ref, sems):
    queries = pltpu.make_async_copy(q_hbm, packed_ref.at[pl.ds(0, TOTAL)], sems.at[0])
    small = [
        pltpu.make_async_copy(mask_hbm, mask_ref, sems.at[1]),
        pltpu.make_async_copy(branch_hbm, branch_ref, sems.at[2]),
    ]
    for copy in small + [queries]:
        copy.start()
    shape = (ROWS, HD)
    lanes = lax.broadcasted_iota(jnp.int32, shape, 1)
    rows = lax.broadcasted_iota(jnp.int32, shape, 0)
    extra = jnp.zeros(shape, jnp.int32)
    for copy in small:
        copy.wait()
    for i in range(KVH):
        extra = jnp.where(lanes == i, mask_ref[:, i : i + 1], extra)
    for r in range(ROWS):
        extra = jnp.where((lanes == KVH) & (rows == r), branch_ref[:, r : r + 1], extra)
    extra = extra.astype(jnp.float32)
    for r in range(ROWS):
        tile = jnp.broadcast_to(extra[r : r + 1, :], (EXT, HD)).astype(jnp.bfloat16)
        packed_ref[TOTAL + r * EXT : TOTAL + (r + 1) * EXT, :] = tile
    queries.wait()


def load_kernel(*refs):
    count = len(refs) // 2
    sems = refs[-1]
    copies = [pltpu.make_async_copy(refs[i], refs[count + i], sems.at[i]) for i in range(count)]
    for copy in copies:
        copy.start()
    for copy in copies:
        copy.wait()


def suffix_kernel(len_ref, q_ref, k_ref, v_ref, out_ref):
    slots = k_ref.shape[1]
    second = ext_column(q_ref, KVH) > 0.5
    wide = jnp.broadcast_to(second, (NQ, HD))
    length = jnp.where(second, len_ref[:, 1:2], len_ref[:, 0:1])
    allowed = lax.broadcasted_iota(jnp.int32, (NQ, slots), 1) < length
    lanes = lax.broadcasted_iota(jnp.int32, (NQ, 128), 1)
    zero = jnp.zeros((NQ, HD), jnp.bfloat16)
    stats = [jnp.zeros((NQ, 128), jnp.float32)]

    def score(j, _):
        query = head_rows(q_ref, j)
        query = jnp.concatenate([jnp.where(wide, zero, query), jnp.where(wide, query, zero)], axis=1)
        return dot_nt(query, jnp.concatenate([k_ref[0, :, head(j)], k_ref[1, :, head(j)]], axis=1))

    def weigh(j, scores):
        return soften([jnp.where(allowed, scores, MASKED)])

    def mix(j, held):
        rounded, largest, mass = held
        mixed = dot_nn(rounded, jnp.concatenate([v_ref[0, :, head(j)], v_ref[1, :, head(j)]], axis=1))
        mixed = jnp.where(second, mixed[:, HD:], mixed[:, :HD])
        store_head(out_ref, j, mixed * (1.0 / mass))
        stats[0] = jnp.where(lanes == j, largest * SCALE + jnp.log2(mass), stats[0])

    pipelined((score, weigh, mix), KVH)
    out_ref[TOTAL : TOTAL + STAT, :] = pack_stats(stats[0])


def prefix_kernel(with_new, *refs):
    q_ref, k_own, v_own, k_near, v_near, k_far, v_far, k_next, v_next = refs[:9]
    if with_new:
        nk_ref, nv_ref, out_ref, stat_ref = refs[9:]
    else:
        (out_ref,) = refs[9:]
    span = lax.axis_index("span")
    core = lax.rem(lax.axis_index("rows"), 2)
    x = lax.rem(span, 4)
    first = span - x
    offsets = (0, 3 + 2 * core, 5 - 2 * core, 2)
    allowed = [ext_column(q_ref, first + lax.rem(x + offset, 4)) > 0.5 for offset in offsets]
    lanes = lax.broadcasted_iota(jnp.int32, (NQ, 128), 1)
    stats = [jnp.zeros((NQ, 128), jnp.float32)]
    if with_new:
        row_of = lax.broadcasted_iota(jnp.int32, (NQ, 128), 0)
        same_row = (row_of // QR) == (lanes // (KVH * STEPS))
        new_base = same_row & ((lanes % STEPS) <= (row_of % STEPS))
        new_head = (lanes // STEPS) % KVH

    def score(j, _):
        keys = [ref[:, head(j)] for ref in (k_own, k_near, k_far, k_next)]
        if with_new:
            keys.append(nk_ref[...])
        return dot_nt(head_rows(q_ref, j), jnp.concatenate(keys, axis=0))

    def weigh(j, scores):
        parts = [jnp.where(allowed[i], scores[:, i * BLK : (i + 1) * BLK], MASKED) for i in range(4)]
        if with_new:
            parts.append(jnp.where(new_base & (new_head == j), scores[:, 4 * BLK :], MASKED))
        return soften(parts)

    def mix(j, held):
        rounded, largest, mass = held
        values = [ref[:, head(j)] for ref in (v_own, v_near, v_far, v_next)]
        if with_new:
            values.append(nv_ref[...])
        mixed = dot_nn(rounded, jnp.concatenate(values, axis=0))
        store_head(out_ref, j, mixed * (1.0 / mass))
        stats[0] = jnp.where(lanes == j, largest * SCALE + jnp.log2(mass), stats[0])

    pipelined((score, weigh, mix), KVH)
    if with_new:
        stat_ref[...] = stats[0]
    else:
        out_ref[TOTAL : TOTAL + STAT, :] = pack_stats(stats[0])


def merge_kernel(own_ref, stat_ref, other_ref, out_ref, *merged_stat):
    own, other = stat_ref[...], unpack_stats(other_ref)
    top = jnp.maximum(own, other)
    mass = jnp.exp2(own - top) + jnp.exp2(other - top)
    share = jnp.exp2(own - top) / mass
    for ref in merged_stat:
        ref[...] = top + jnp.log2(mass)
    for j in range(KVH):
        for r in range(ROWS):
            rows = slice(r * 256 + j * QR, r * 256 + (j + 1) * QR)
            second = other_ref[rows, :].astype(jnp.float32)
            weight = share[r * QR : (r + 1) * QR, j : j + 1]
            out_ref[rows, :] = (second + (own_ref[rows, :] - second) * weight).astype(out_ref.dtype)


VMEM = pl.BlockSpec(memory_space=pltpu.VMEM)
HBM = pl.BlockSpec(memory_space=pltpu.HBM)


def vmem(shape, dtype=jnp.bfloat16):
    return pltpu.VMEM(shape, dtype)


PACKED = vmem((TOTAL + STAT, HD))


def in_hbm(*values):
    return tuple(pltpu.with_memory_space_constraint(value, pltpu.HBM) for value in values)


def call(kernel, args, specs, out, scratch=()):
    return pl.pallas_call(
        kernel,
        out_shape=out,
        in_specs=specs,
        out_specs=jax.tree.map(lambda _: VMEM, out),
        scratch_shapes=list(scratch),
        cost_estimate=pl.CostEstimate(flops=1, bytes_accessed=1, transcendentals=0),
        compiler_params=pltpu.CompilerParams(vmem_limit_bytes=16 << 20),
    )(*args)


def heads_first(value, heads):
    rows, steps, _ = value.shape
    return value.reshape(rows, steps, heads, HD).transpose(0, 2, 1, 3).reshape(rows * heads * steps, HD)


def on_device(
    queries,
    prefix_keys,
    prefix_values,
    prefix_mask,
    suffix_keys,
    suffix_values,
    suffix_len,
    row_branch,
    new_keys,
    new_values,
):
    packed = call(
        pack_kernel,
        in_hbm(heads_first(queries, H), prefix_mask, row_branch.reshape(1, ROWS)),
        [HBM] * 3,
        vmem((TOTAL + ROWS * EXT, HD)),
        [
            pltpu.VMEM(prefix_mask.shape, jnp.int32),
            pltpu.VMEM((1, ROWS), jnp.int32),
            pltpu.SemaphoreType.DMA((3,)),
        ],
    )
    k_near = send(prefix_keys, along_x)
    far_queries = send(packed, to_partner)
    v_near = send(after(prefix_values, packed), along_x)
    stored = call(
        load_kernel,
        in_hbm(*after((suffix_len.reshape(1, 2), suffix_keys, suffix_values), packed)),
        [HBM] * 3,
        (vmem((1, 2), jnp.int32), vmem(suffix_keys.shape), vmem(suffix_values.shape)),
        [pltpu.SemaphoreType.DMA((3,))],
    )
    k_next = send(after(k_near, stored[0]), along_x)
    v_next = send(after(v_near, stored[0]), along_x)
    k_far = send(after(k_near, stored[0]), other_core)
    v_far = send(after(v_near, stored[0]), other_core)
    near_queries = send(after(packed, k_near, stored[0]), to_neighbour)
    far_queries = after(far_queries, k_far)
    suffix = call(suffix_kernel, (stored[0], far_queries, stored[1], stored[2]), [VMEM] * 4, PACKED)
    suffix = send(suffix, to_partner)

    blocks = (prefix_keys, prefix_values, k_near, v_near, k_far, v_far, k_next, v_next)
    near = call(functools.partial(prefix_kernel, False), (near_queries,) + blocks, [VMEM] * 9, PACKED)
    near = send(near, from_neighbour)
    partial = (vmem((TOTAL, HD), jnp.float32), vmem((NQ, 128), jnp.float32))
    own, stat = call(
        functools.partial(prefix_kernel, True),
        (packed,) + blocks + (heads_first(new_keys, KVH), heads_first(new_values, KVH)),
        [VMEM] * 11,
        partial,
    )
    own, stat = call(merge_kernel, (own, stat, suffix), [VMEM] * 3, partial)
    merged = call(merge_kernel, (own, stat, near), [VMEM] * 3, jax.ShapeDtypeStruct((TOTAL, HD), jnp.bfloat16))
    merged = merged.reshape(ROWS, H, STEPS, HD).transpose(0, 2, 1, 3)
    return merged.reshape(queries.shape)


def solution(mesh):
    return jax.shard_map(
        on_device,
        mesh=mesh,
        in_specs=(
            P(AXES, None, None),
            P("span", None),
            P("span", None),
            P(AXES, None),
            P(AXES, None, None),
            P(AXES, None, None),
            P(AXES),
            P(AXES),
            P(AXES, None, None),
            P(AXES, None, None),
        ),
        out_specs=P(AXES, None, None),
        check_vma=False,
    )
```

```python
import functools

import jax
import jax.numpy as jnp
from jax import lax
from jax.experimental import pallas as pl
from jax.experimental.pallas import tpu as pltpu
from jax.sharding import PartitionSpec as P

H = 64
KVH = 8
HD = 128
BLK = 128
GROUP = H // KVH
AXES = ("span", "rows")
MASKED = -1e30
SCALE = 1.4426950408889634 * HD ** (-0.5)
ROWS = 4
STEPS = 4
QR = GROUP * STEPS
NQ = ROWS * QR
TOTAL = KVH * NQ
EXT = 16
STAT = 32


def device_id(x, y, z, c):
    x, y, z, c = x % 4, y % 4, z % 8, c % 2
    return ((y % 2) * 4 + x) * 32 + (y // 2) * 16 + z * 2 + c


def send(value, target):
    pairs = [
        (device_id(x, y, z, c), device_id(*target(x, y, z, c)))
        for x in range(4)
        for y in range(4)
        for z in range(8)
        for c in range(2)
    ]
    return lax.ppermute(value, AXES, pairs)


def after(value, *others):
    return lax.optimization_barrier((value, *others))[0]


def to_partner(x, y, z, c):
    return (x, y + 2, z, c)


def to_neighbour(x, y, z, c):
    return (x, y + 1 - 2 * c, z, c)


def from_neighbour(x, y, z, c):
    return (x, y - 1 + 2 * c, z, c)


def along_x(x, y, z, c):
    return (x + 1 - 2 * c, y, z, c)


def other_core(x, y, z, c):
    return (x, y, z, 1 - c)


def dot_nt(a, b):
    return lax.dot_general(a, b, (((1,), (1,)), ((), ())), preferred_element_type=jnp.float32)


def dot_nn(a, b):
    return lax.dot_general(a, b, (((1,), (0,)), ((), ())), preferred_element_type=jnp.float32)


def head_rows(ref, j):
    return jnp.concatenate([ref[r * 256 + j * QR : r * 256 + (j + 1) * QR, :] for r in range(ROWS)], axis=0)


def ext_column(q_ref, lane):
    ext = q_ref[TOTAL : TOTAL + EXT, :].astype(jnp.float32)
    lanes = lax.broadcasted_iota(jnp.int32, ext.shape, 1)
    column = jnp.sum(jnp.where(lanes == lane, ext, 0.0), axis=1, keepdims=True)
    each = EXT // ROWS
    return jnp.concatenate([jnp.broadcast_to(column[r * each : r * each + 1, :], (QR, 1)) for r in range(ROWS)], axis=0)


def pack_stats(stat):
    rows = stat.T[:KVH, :]
    hi = rows.astype(jnp.bfloat16)
    rest = rows - hi.astype(jnp.float32)
    mid = rest.astype(jnp.bfloat16)
    low = (rest - mid.astype(jnp.float32)).astype(jnp.bfloat16)
    pad = jnp.zeros_like(hi)
    return jnp.concatenate([hi, mid, low, pad], axis=0)


def unpack_stats(ref):
    rows = ref[TOTAL : TOTAL + STAT, :].astype(jnp.float32)
    rows = rows[:KVH] + rows[KVH : 2 * KVH] + rows[2 * KVH : 3 * KVH]
    full = jnp.concatenate([rows, jnp.zeros((NQ - KVH, NQ), jnp.float32)], axis=0)
    return full.T


def pipelined(stages, count):
    held = {}
    for time in range(count + len(stages) - 1):
        for s in range(len(stages)):
            i = time - s
            if 0 <= i < count:
                held[i] = stages[s](i, held.get(i))


def soften(parts):
    largest = jnp.max(functools.reduce(jnp.maximum, parts), axis=1, keepdims=True)
    weights = [jnp.exp2((part - largest) * SCALE) for part in parts]
    mass = jnp.sum(functools.reduce(jnp.add, weights), axis=1, keepdims=True)
    rounded = jnp.concatenate([w.astype(jnp.bfloat16) for w in weights], axis=1)
    return rounded, largest, mass


def store_head(out_ref, j, result):
    for r in range(ROWS):
        out_ref[r * 256 + j * QR : r * 256 + (j + 1) * QR, :] = result[r * QR : (r + 1) * QR, :].astype(out_ref.dtype)


def head(j):
    return slice(j * HD, (j + 1) * HD)


def pack_kernel(q_hbm, mask_hbm, branch_hbm, packed_ref, mask_ref, branch_ref, sems):
    queries = pltpu.make_async_copy(q_hbm, packed_ref.at[pl.ds(0, TOTAL)], sems.at[0])
    small = [
        pltpu.make_async_copy(mask_hbm, mask_ref, sems.at[1]),
        pltpu.make_async_copy(branch_hbm, branch_ref, sems.at[2]),
    ]
    for copy in small + [queries]:
        copy.start()
    shape = (ROWS, HD)
    lanes = lax.broadcasted_iota(jnp.int32, shape, 1)
    rows = lax.broadcasted_iota(jnp.int32, shape, 0)
    extra = jnp.zeros(shape, jnp.int32)
    for copy in small:
        copy.wait()
    for i in range(KVH):
        extra = jnp.where(lanes == i, mask_ref[:, i : i + 1], extra)
    for r in range(ROWS):
        extra = jnp.where((lanes == KVH) & (rows == r), branch_ref[:, r : r + 1], extra)
    extra = extra.astype(jnp.float32)
    tile = [jnp.broadcast_to(extra[r : r + 1, :], (EXT // ROWS, HD)) for r in range(ROWS)]
    packed_ref[TOTAL : TOTAL + EXT, :] = jnp.concatenate(tile, axis=0).astype(jnp.bfloat16)
    queries.wait()


def load_kernel(*refs):
    count = len(refs) // 2
    sems = refs[-1]
    copies = [pltpu.make_async_copy(refs[i], refs[count + i], sems.at[i]) for i in range(count)]
    for copy in copies:
        copy.start()
    for copy in copies:
        copy.wait()


def suffix_kernel(len_ref, q_ref, k_ref, v_ref, out_ref):
    slots = k_ref.shape[1]
    second = ext_column(q_ref, KVH) > 0.5
    wide = jnp.broadcast_to(second, (NQ, HD))
    length = jnp.where(second, len_ref[:, 1:2], len_ref[:, 0:1])
    allowed = lax.broadcasted_iota(jnp.int32, (NQ, slots), 1) < length
    lanes = lax.broadcasted_iota(jnp.int32, (NQ, 128), 1)
    zero = jnp.zeros((NQ, HD), jnp.bfloat16)
    stats = [jnp.zeros((NQ, 128), jnp.float32)]

    def score(j, _):
        query = head_rows(q_ref, j)
        query = jnp.concatenate([jnp.where(wide, zero, query), jnp.where(wide, query, zero)], axis=1)
        return dot_nt(query, jnp.concatenate([k_ref[0, :, head(j)], k_ref[1, :, head(j)]], axis=1))

    def weigh(j, scores):
        return soften([jnp.where(allowed, scores, MASKED)])

    def mix(j, held):
        rounded, largest, mass = held
        mixed = dot_nn(rounded, jnp.concatenate([v_ref[0, :, head(j)], v_ref[1, :, head(j)]], axis=1))
        mixed = jnp.where(second, mixed[:, HD:], mixed[:, :HD])
        store_head(out_ref, j, mixed * (1.0 / mass))
        stats[0] = jnp.where(lanes == j, largest * SCALE + jnp.log2(mass), stats[0])

    pipelined((score, weigh, mix), KVH)
    out_ref[TOTAL : TOTAL + STAT, :] = pack_stats(stats[0])


def prefix_kernel(with_new, *refs):
    q_ref, k_own, v_own, k_near, v_near, k_far, v_far, k_next, v_next = refs[:9]
    if with_new:
        nk_ref, nv_ref, out_ref, stat_ref = refs[9:]
    else:
        (out_ref,) = refs[9:]
    span = lax.axis_index("span")
    core = lax.rem(lax.axis_index("rows"), 2)
    x = lax.rem(span, 4)
    first = span - x
    offsets = (0, 3 + 2 * core, 5 - 2 * core, 2)
    allowed = [ext_column(q_ref, first + lax.rem(x + offset, 4)) > 0.5 for offset in offsets]
    lanes = lax.broadcasted_iota(jnp.int32, (NQ, 128), 1)
    stats = [jnp.zeros((NQ, 128), jnp.float32)]
    if with_new:
        row_of = lax.broadcasted_iota(jnp.int32, (NQ, 128), 0)
        same_row = (row_of // QR) == (lanes // (KVH * STEPS))
        new_base = same_row & ((lanes % STEPS) <= (row_of % STEPS))
        new_head = (lanes // STEPS) % KVH

    def score(j, _):
        keys = [ref[:, head(j)] for ref in (k_own, k_near, k_far, k_next)]
        if with_new:
            keys.append(nk_ref[...])
        return dot_nt(head_rows(q_ref, j), jnp.concatenate(keys, axis=0))

    def weigh(j, scores):
        parts = [jnp.where(allowed[i], scores[:, i * BLK : (i + 1) * BLK], MASKED) for i in range(4)]
        if with_new:
            parts.append(jnp.where(new_base & (new_head == j), scores[:, 4 * BLK :], MASKED))
        return soften(parts)

    def mix(j, held):
        rounded, largest, mass = held
        values = [ref[:, head(j)] for ref in (v_own, v_near, v_far, v_next)]
        if with_new:
            values.append(nv_ref[...])
        mixed = dot_nn(rounded, jnp.concatenate(values, axis=0))
        store_head(out_ref, j, mixed * (1.0 / mass))
        stats[0] = jnp.where(lanes == j, largest * SCALE + jnp.log2(mass), stats[0])

    pipelined((score, weigh, mix), KVH)
    if with_new:
        stat_ref[...] = stats[0]
    else:
        out_ref[TOTAL : TOTAL + STAT, :] = pack_stats(stats[0])


def merge_kernel(own_ref, stat_ref, other_ref, out_ref, *merged_stat):
    own, other = stat_ref[...], unpack_stats(other_ref)
    top = jnp.maximum(own, other)
    mass = jnp.exp2(own - top) + jnp.exp2(other - top)
    share = jnp.exp2(own - top) / mass
    for ref in merged_stat:
        ref[...] = top + jnp.log2(mass)
    for j in range(KVH):
        for r in range(ROWS):
            rows = slice(r * 256 + j * QR, r * 256 + (j + 1) * QR)
            second = other_ref[rows, :].astype(jnp.float32)
            weight = share[r * QR : (r + 1) * QR, j : j + 1]
            out_ref[rows, :] = (second + (own_ref[rows, :] - second) * weight).astype(out_ref.dtype)


VMEM = pl.BlockSpec(memory_space=pltpu.VMEM)
HBM = pl.BlockSpec(memory_space=pltpu.HBM)


def vmem(shape, dtype=jnp.bfloat16):
    return pltpu.VMEM(shape, dtype)


PACKED = vmem((TOTAL + STAT, HD))


def in_hbm(*values):
    return tuple(pltpu.with_memory_space_constraint(value, pltpu.HBM) for value in values)


def call(kernel, args, specs, out, scratch=()):
    return pl.pallas_call(
        kernel,
        out_shape=out,
        in_specs=specs,
        out_specs=jax.tree.map(lambda _: VMEM, out),
        scratch_shapes=list(scratch),
        cost_estimate=pl.CostEstimate(flops=1, bytes_accessed=1, transcendentals=0),
        compiler_params=pltpu.CompilerParams(vmem_limit_bytes=16 << 20),
    )(*args)


def heads_first(value, heads):
    rows, steps, _ = value.shape
    return value.reshape(rows, steps, heads, HD).transpose(0, 2, 1, 3).reshape(rows * heads * steps, HD)


def on_device(
    queries,
    prefix_keys,
    prefix_values,
    prefix_mask,
    suffix_keys,
    suffix_values,
    suffix_len,
    row_branch,
    new_keys,
    new_values,
):
    packed = call(
        pack_kernel,
        in_hbm(heads_first(queries, H), prefix_mask, row_branch.reshape(1, ROWS)),
        [HBM] * 3,
        vmem((TOTAL + EXT, HD)),
        [
            pltpu.VMEM(prefix_mask.shape, jnp.int32),
            pltpu.VMEM((1, ROWS), jnp.int32),
            pltpu.SemaphoreType.DMA((3,)),
        ],
    )
    k_near = send(prefix_keys, along_x)
    far_queries = send(packed, to_partner)
    v_near = send(after(prefix_values, packed), along_x)
    stored = call(
        load_kernel,
        in_hbm(*after((suffix_len.reshape(1, 2), suffix_keys, suffix_values), packed)),
        [HBM] * 3,
        (vmem((1, 2), jnp.int32), vmem(suffix_keys.shape), vmem(suffix_values.shape)),
        [pltpu.SemaphoreType.DMA((3,))],
    )
    k_next = send(after(k_near, stored[0]), along_x)
    v_next = send(after(v_near, stored[0]), along_x)
    k_far = send(after(k_near, stored[0]), other_core)
    v_far = send(after(v_near, stored[0]), other_core)
    near_queries = send(after(packed, k_near, stored[0]), to_neighbour)
    far_queries = after(far_queries, k_far)
    suffix = call(suffix_kernel, (stored[0], far_queries, stored[1], stored[2]), [VMEM] * 4, PACKED)
    suffix = send(suffix, to_partner)

    blocks = (prefix_keys, prefix_values, k_near, v_near, k_far, v_far, k_next, v_next)
    near = call(functools.partial(prefix_kernel, False), (near_queries,) + blocks, [VMEM] * 9, PACKED)
    near = send(near, from_neighbour)
    partial = (vmem((TOTAL, HD), jnp.float32), vmem((NQ, 128), jnp.float32))
    own, stat = call(
        functools.partial(prefix_kernel, True),
        (packed,) + blocks + (heads_first(new_keys, KVH), heads_first(new_values, KVH)),
        [VMEM] * 11,
        partial,
    )
    own, stat = call(merge_kernel, (own, stat, suffix), [VMEM] * 3, partial)
    merged = call(merge_kernel, (own, stat, near), [VMEM] * 3, jax.ShapeDtypeStruct((TOTAL, HD), jnp.bfloat16))
    merged = merged.reshape(ROWS, H, STEPS, HD).transpose(0, 2, 1, 3)
    return merged.reshape(queries.shape)


def solution(mesh):
    return jax.shard_map(
        on_device,
        mesh=mesh,
        in_specs=(
            P(AXES, None, None),
            P("span", None),
            P("span", None),
            P(AXES, None),
            P(AXES, None, None),
            P(AXES, None, None),
            P(AXES),
            P(AXES),
            P(AXES, None, None),
            P(AXES, None, None),
        ),
        out_specs=P(AXES, None, None),
        check_vma=False,
    )
```
